512 devices in a mesh: blk: 8 (over y), uly: 8 (over x, core), tp: 8 (over z).
Axes of the slice: x: 4, y: 8, z: 8, core: 2. Of those that a mesh axis runs over, the one named last changes fastest.
Arguments:
- queries: bfloat16 [8192, 64, 128], P(('blk', 'uly'), 'tp'), may hold values from -84 to 84
- keys: bfloat16 [8192, 8, 128], P(('blk', 'uly'), 'tp'), may hold values from -12 to 12
- values: bfloat16 [8192, 8, 128], P(('blk', 'uly'), 'tp'), may hold values from -6 to 6
- span_order: int32 [16], replicated, may hold values from 0 to 15, each once
Outputs:
- attended: bfloat16 [8192, 64, 128], P(('blk', 'uly'), 'tp')
The draws below stay inside these ranges and needn't reach their ends.
Inputs may be any that keep to these rules, and one draw needn't show every extreme that they name: `span_order`: holds every number from 0 to 15 exactly once.
All inputs are finite; a program needn't handle non-finite values.
Results may differ from the reference program's by a relative error of at most 0.0065.
Values may be sent and summed in bfloat16 or wider, within the bound.
No kernel may reach another device: no remote copies, remote signals or barrier semaphores. Data moves between devices by JAX's collectives and lax.ppermute only.
A program may use at most 64 MiB of HBM per device.

```python
import math
import jax
import jax.numpy as jnp
from jax import lax

QUERY_HEAD_COUNT = 64
KEY_VALUE_HEADS = 8
HEAD_DIM = 128
SEQUENCE_TOKENS = 8192
NCHUNK = 16


def key_column_field(key):
    gaussian_draw_part = jax.random.truncated_normal(jax.random.fold_in(key, 11), -6.0, 6.0, (SEQUENCE_TOKENS, KEY_VALUE_HEADS, HEAD_DIM), jnp.float32)
    return gaussian_draw_part


def draw_keys(key, part):
    return key_column_field(key).astype(jnp.bfloat16)


def draw_queries(key, part):
    gaussian_draw_part = jax.random.truncated_normal(jax.random.fold_in(key, 23), -6.0, 6.0, (SEQUENCE_TOKENS, QUERY_HEAD_COUNT, HEAD_DIM), jnp.float32)
    return gaussian_draw_part.astype(jnp.bfloat16)


def block_scale(rng, dims, shards, least, top_value):
    level, own = 1.0, jax.random.fold_in(rng, 6)
    for dim, parts in shards:
        steps = jnp.exp(jax.random.uniform(jax.random.fold_in(own, dim), (parts,), jnp.float32, least / len(shards), top_value / len(shards)))
        level = level * jnp.repeat(steps, dims[dim] // parts).reshape([-1 if axis == dim else 1 for axis in range(len(dims))])
    return level


def bell_draw(key, dims, width, most, shards=(), kind=jnp.bfloat16):
    drawn = jax.random.normal(key, dims, jnp.float32) * width
    if len(shards) > 0:
        drawn = block_scale(key, dims, shards, -0.22, 0.18) * drawn
    return jnp.clip(drawn, min=-most, max=most).astype(kind)


def setup_inputs(seed: int = 0) -> dict:
    key_of = jax.random.split(jax.random.key(seed), 5)
    queries = draw_queries(jax.random.fold_in(key_of[4], 71), 0)
    keys = draw_keys(jax.random.fold_in(key_of[4], 71), 0)
    values = bell_draw(key_of[2], (SEQUENCE_TOKENS, KEY_VALUE_HEADS, HEAD_DIM), 1.0, 6.0, ((0, 64), (1, 8)))
    span_order = jax.random.permutation(key_of[3], NCHUNK).astype(jnp.int32)
    return {"queries": queries, "keys": keys, "values": values, "span_order": span_order}


def span_positions(row_index, span_order, span_len):
    span_index = row_index // span_len
    span_ids = jnp.arange(span_order.shape[0], dtype=jnp.int32)
    span_hit = span_index[:, None] == span_ids[None, :]
    start_pos = lax.optimization_barrier(jnp.sum(jnp.where(span_hit, span_order[None, :], 0), axis=1)).astype(jnp.int32)
    return start_pos * span_len + row_index % span_len

def reference(queries, keys, values, span_order):
    span_len = SEQUENCE_TOKENS // NCHUNK
    positions = span_positions(jnp.arange(SEQUENCE_TOKENS, dtype=jnp.int32), span_order, span_len)
    visible = positions[None, :] <= positions[:, None]
    score_scale = 1.0 / math.sqrt(HEAD_DIM)
    query_group_width = QUERY_HEAD_COUNT // KEY_VALUE_HEADS
    query_heads = jnp.moveaxis(queries, 1, 0)
    key_heads = jnp.moveaxis(keys, 1, 0)
    value_heads = jnp.moveaxis(values, 1, 0)

    def one_head(inputs):
        query_block, head_number = inputs
        kv_number = (head_number // query_group_width).astype(jnp.int32)
        key_block = lax.dynamic_index_in_dim(key_heads, kv_number, 0, keepdims=False)
        value_block = lax.dynamic_index_in_dim(value_heads, kv_number, 0, keepdims=False)
        scores = jnp.dot(query_block, key_block.T, preferred_element_type=jnp.float32) * score_scale
        scores = jnp.where(visible, scores, -1e+30)
        row_max = lax.optimization_barrier(jnp.max(scores, axis=1))
        weights = jnp.where(visible, jnp.exp(scores - row_max[:, None]), 0.0)
        row_sum = lax.optimization_barrier(jnp.sum(weights, axis=1))
        mixed = jnp.dot(weights.astype(jnp.bfloat16), value_block, preferred_element_type=jnp.float32)
        return (mixed / row_sum[:, None]).astype(jnp.bfloat16)
    attended = lax.map(one_head, (query_heads, jnp.arange(QUERY_HEAD_COUNT, dtype=jnp.int32)))
    return jnp.moveaxis(attended, 0, 1)
```

```python
import math

import jax
import jax.numpy as jnp
from jax import lax
from jax.experimental import pallas as pl
from jax.experimental.pallas import tpu as pltpu
from jax.sharding import Mesh, PartitionSpec as P

LOG2E = 1.4426950408889634
MASKED = -1.5e38
START = -1.0e30
ROW_BLOCK = 256


def attend_kernel(first, last, peers, rows, heads, info, q_ref, kv_ref, *refs):
    if not first:
        m_in, l_in, a_in, *refs = refs
    if last:
        out_ref, m_ref, l_ref, a_ref = refs
    else:
        m_ref, l_ref, a_ref = refs
    if first:
        m_ref[...] = jnp.full(m_ref.shape, START, jnp.float32)
        l_ref[...] = jnp.zeros(l_ref.shape, jnp.float32)
        a_ref[...] = jnp.zeros(a_ref.shape, jnp.float32)
    else:
        m_ref[...] = m_in[...]
        l_ref[...] = l_in[...]
        a_ref[...] = a_in[...]
    total_rows, head_size = q_ref.shape
    spans = 16
    per_span = peers // spans
    keys = per_span * rows
    own_span = info[spans]
    query_start = info[spans + 1]
    key_start = info[spans + 2]
    factor = LOG2E / math.sqrt(head_size)

    def fold(j, diagonal):
        block = kv_ref[pl.ds(j * per_span, per_span)]
        k = block[:, :rows].reshape(keys, head_size)
        v = block[:, rows:].reshape(keys, head_size)
        for r in range(0, total_rows, ROW_BLOCK):
            at = pl.ds(r, ROW_BLOCK)
            s = lax.dot_general(
                q_ref[at, :], k, (((1,), (1,)), ((), ())), preferred_element_type=jnp.float32
            ) * factor
            if diagonal:
                row = lax.broadcasted_iota(jnp.int32, s.shape, 0) + r
                col = lax.broadcasted_iota(jnp.int32, s.shape, 1)
                q_off = query_start + row // heads
                k_off = key_start + (col // rows) * (2 * rows) + col % rows
                s = jnp.where(k_off <= q_off, s, MASKED)
            m_old = m_ref[at, :]
            m_new = jnp.maximum(m_old, jnp.max(s, axis=1, keepdims=True))
            alpha = jnp.exp2(m_old - m_new)
            p = jnp.exp2(s - jnp.tile(m_new, (1, keys // 128)))
            part = p[:, :128]
            for c in range(128, keys, 128):
                part = part + p[:, c : c + 128]
            m_ref[at, :] = m_new
            l_ref[at, :] = l_ref[at, :] * alpha + part
            a_ref[at, :] = a_ref[at, :] * alpha + jnp.dot(
                p.astype(jnp.bfloat16), v, preferred_element_type=jnp.float32
            )

    @pl.loop(0, spans)
    def _(j):
        here = info[j]

        @pl.when(here < own_span)
        def _():
            fold(j, False)

        @pl.when(here == own_span)
        def _():
            fold(j, True)

    if last:
        total = jnp.sum(l_ref[...], axis=1, keepdims=True)
        out_ref[...] = (a_ref[...] / total).astype(jnp.bfloat16)


def attend(info, q, kv, state, last, rows, heads):
    total_rows, head_size = q.shape
    peers = kv.shape[0]
    vm = pl.BlockSpec(memory_space=pltpu.VMEM)
    stat = jax.ShapeDtypeStruct((total_rows, 128), jnp.float32)
    acc = jax.ShapeDtypeStruct((total_rows, head_size), jnp.float32)
    first = state is None
    args = [info, q, kv] + ([] if first else list(state))
    shapes = [stat, stat, acc]
    if last:
        out_shape = jax.ShapeDtypeStruct((total_rows, head_size), jnp.bfloat16)
        out_specs = vm
        scratch = [pltpu.VMEM(s.shape, s.dtype) for s in shapes]
    else:
        out_shape, out_specs, scratch = shapes, [vm] * 3, []

    def body(*refs):
        attend_kernel(first, last, peers, rows, heads, *refs)

    keys = peers * rows
    return pl.pallas_call(
        body,
        out_shape=out_shape,
        in_specs=[pl.BlockSpec(memory_space=pltpu.SMEM)] + [vm] * (len(args) - 1),
        out_specs=out_specs,
        scratch_shapes=scratch,
        compiler_params=pltpu.CompilerParams(vmem_limit_bytes=40 * 1024 * 1024),
        cost_estimate=pl.CostEstimate(
            flops=4 * total_rows * keys * head_size,
            bytes_accessed=4 * keys * head_size + 2 * total_rows * head_size,
            transcendentals=total_rows * keys,
        ),
    )(*args)


def local(queries, keys, values, span_order):
    rows, heads, head_size = queries.shape
    blk, x, core = lax.axis_index("blk"), lax.axis_index("x"), lax.axis_index("core")
    across = lax.axis_size("blk") * lax.axis_size("x")
    q = queries.reshape(rows * heads, head_size)
    kv = jnp.concatenate([keys.reshape(rows, head_size), values.reshape(rows, head_size)], axis=0)
    place = blk * 2 + x // 2
    own_span = jnp.sum(jnp.where(jnp.arange(16) == place, span_order, 0))
    query_start = (x % 2) * (2 * rows) + core * rows

    def info(which):
        return jnp.concatenate(
            [span_order, jnp.stack([own_span, query_start, which * rows]).astype(jnp.int32)]
        )

    copies = jnp.broadcast_to(kv[None], (across, 2 * rows, head_size))
    mine = lax.all_to_all(copies, ("blk", "x"), 0, 0, tiled=True)
    other = lax.ppermute(mine, "core", [(0, 1), (1, 0)])
    state = attend(info(core), q, mine, None, False, rows, heads)
    out = attend(info(1 - core), q, other, state, True, rows, heads)
    return out.reshape(rows, heads, head_size)


def solution(mesh):
    blk, uly, tp = mesh.devices.shape
    fine = Mesh(mesh.devices.reshape(blk, uly // 2, 2, tp), ("blk", "x", "core", "tp"))
    spec = P(("blk", "x", "core"), "tp", None)
    return jax.shard_map(
        local, mesh=fine, in_specs=(spec, spec, spec, P()), out_specs=spec, check_vma=False
    )
```

```python
import math

import jax
import jax.numpy as jnp
from jax import lax
from jax.experimental import pallas as pl
from jax.experimental.pallas import tpu as pltpu
from jax.sharding import Mesh, PartitionSpec as P

LOG2E = 1.4426950408889634
MASKED = -1.5e38
START = -1.0e30
FAR = 1 << 20
SPANS = 16
GROUP = 8
COLUMNS = 1024
VMEM_BYTES = 40 * 1024 * 1024


def prepare_kernel(q_ref, t_ref):
    head_size = q_ref.shape[1]
    scaled = q_ref[...].astype(jnp.float32).T * (LOG2E / math.sqrt(head_size))
    high = scaled.astype(jnp.bfloat16)
    t_ref[:head_size, :] = high
    t_ref[head_size:, :] = (scaled - high.astype(jnp.float32)).astype(jnp.bfloat16)


def prepare(q):
    vm = pl.BlockSpec(memory_space=pltpu.VMEM)
    return pl.pallas_call(
        prepare_kernel,
        out_shape=jax.ShapeDtypeStruct((2 * q.shape[1], q.shape[0]), q.dtype),
        in_specs=[vm],
        out_specs=vm,
        compiler_params=pltpu.CompilerParams(vmem_limit_bytes=VMEM_BYTES),
    )(q)


def attend_kernel(count, first, last, heads, info, q_ref, kv_ref, *refs):
    if not first:
        m_in, l_in, a_in, *refs = refs
    if last:
        out_ref, m_ref, l_ref, a_ref, seen, base = refs
    else:
        m_ref, l_ref, a_ref, seen, base = refs
    if first:
        m_ref[...] = jnp.full(m_ref.shape, START, jnp.float32)
        l_ref[...] = jnp.zeros(l_ref.shape, jnp.float32)
        a_ref[...] = jnp.zeros(a_ref.shape, jnp.float32)
    else:
        m_ref[...] = m_in[...]
        l_ref[...] = l_in[...]
        a_ref[...] = a_in[...]
    total = q_ref.shape[1]
    rows = kv_ref.shape[1] // 2
    query_start = info[0]

    for i in range(count + GROUP):
        seen[i] = 0
        base[i] = FAR
    free = jnp.int32(0)
    for e in range(count):
        seen[free] = e
        base[free] = -FAR
        free = free + (info[1 + 2 * e] == 1).astype(jnp.int32)
    full = free // GROUP
    for e in range(count):
        own = info[1 + 2 * e] == 2
        seen[free] = e
        base[free] = jnp.where(own, info[2 + 2 * e], FAR)
        free = free + own.astype(jnp.int32)
    base[free] = FAR

    def fold(g, masked):
        blocks = [kv_ref[pl.ds(seen[g * GROUP + i], 1)] for i in range(GROUP)]
        k = jnp.concatenate([b[0, :rows] for b in blocks], axis=0)
        v = jnp.concatenate([b[0, rows:] for b in blocks], axis=0)
        k = jnp.concatenate([k, k], axis=1)
        for c in range(0, total, COLUMNS):
            at = pl.ds(c, COLUMNS)
            s = jnp.dot(k, q_ref[:, at], preferred_element_type=jnp.float32)
            if masked:
                shape = (rows, COLUMNS)
                offset = query_start + (lax.broadcasted_iota(jnp.int32, shape, 1) + c) // heads
                gap = offset - lax.broadcasted_iota(jnp.int32, shape, 0)
                s = jnp.concatenate(
                    [
                        jnp.where(gap >= base[g * GROUP + i], s[i * rows : (i + 1) * rows], MASKED)
                        for i in range(GROUP)
                    ],
                    axis=0,
                )
            m_old = m_ref[:, at]
            m_new = jnp.maximum(m_old, jnp.max(s, axis=0, keepdims=True))
            alpha = jnp.exp2(m_old - m_new)
            p = jnp.exp2(s - m_new)
            m_ref[:, at] = m_new
            l_ref[:, at] = l_ref[:, at] * alpha + jnp.sum(p, axis=0, keepdims=True)
            a_ref[:, at] = a_ref[:, at] * alpha + lax.dot_general(
                v,
                p.astype(jnp.bfloat16),
                (((0,), (0,)), ((), ())),
                preferred_element_type=jnp.float32,
            )

    @pl.loop(0, full)
    def _(g):
        fold(g, False)

    @pl.loop(full, (free + GROUP - 1) // GROUP)
    def _(g):
        fold(g, True)

    if last:
        out_ref[...] = (a_ref[...] / l_ref[...]).T.astype(jnp.bfloat16)


def attend(info, q, kv, state, last, heads):
    total = q.shape[1]
    count, both_rows, head_size = kv.shape
    vm = pl.BlockSpec(memory_space=pltpu.VMEM)
    stat = jax.ShapeDtypeStruct((1, total), jnp.float32)
    acc = jax.ShapeDtypeStruct((head_size, total), jnp.float32)
    first = state is None
    args = [info, q, kv] + ([] if first else list(state))
    shapes = [stat, stat, acc]
    lists = [pltpu.SMEM((count + GROUP + 1,), jnp.int32)] * 2
    if last:
        out_shape = jax.ShapeDtypeStruct((total, head_size), jnp.bfloat16)
        out_specs = vm
        scratch = [pltpu.VMEM(s.shape, s.dtype) for s in shapes] + lists
    else:
        out_shape, out_specs, scratch = shapes, [vm] * 3, lists

    def body(*refs):
        attend_kernel(count, first, last, heads, *refs)

    keys = count * both_rows // 2
    return pl.pallas_call(
        body,
        out_shape=out_shape,
        in_specs=[pl.BlockSpec(memory_space=pltpu.SMEM)] + [vm] * (len(args) - 1),
        out_specs=out_specs,
        scratch_shapes=scratch,
        compiler_params=pltpu.CompilerParams(vmem_limit_bytes=VMEM_BYTES),
        cost_estimate=pl.CostEstimate(
            flops=4 * total * keys * head_size,
            bytes_accessed=4 * keys * head_size + 2 * total * head_size,
            transcendentals=total * keys,
        ),
    )(*args)


def local(queries, keys, values, span_order):
    rows, heads, head_size = queries.shape
    blk, x, core = lax.axis_index("blk"), lax.axis_index("x"), lax.axis_index("core")
    down, across = lax.axis_size("blk"), lax.axis_size("x")
    per_span = across // 2
    q = prepare(queries.reshape(rows * heads, head_size))
    kv = jnp.concatenate([keys.reshape(rows, head_size), values.reshape(rows, head_size)], axis=0)
    hit = jnp.arange(SPANS, dtype=jnp.int32) == 2 * blk + x // per_span
    own_span = jnp.sum(jnp.where(hit, span_order, 0))
    kinds = jnp.where(span_order < own_span, 1, jnp.where(span_order == own_span, 2, 0))
    kinds = kinds.reshape(down, 2).T[jnp.arange(across) // per_span]
    column = jnp.arange(across, dtype=jnp.int32)

    def info(which, columns, kinds):
        starts = (columns % per_span) * (2 * rows) + which * rows
        starts = jnp.broadcast_to(starts[:, None], kinds.shape)
        query_start = (x % per_span) * (2 * rows) + core * rows
        pairs = jnp.stack([kinds, starts], axis=2).reshape(-1)
        return jnp.concatenate([query_start[None], pairs]).astype(jnp.int32)

    here = column == x
    own_kinds = jnp.sum(jnp.where(here[:, None], kinds, 0), axis=0, keepdims=True)
    other_kinds = jnp.where(here[:, None], 0, kinds)
    swap = [(0, 1), (1, 0)]

    copies = jnp.broadcast_to(kv[None], (down, 2 * rows, head_size))
    mine = lax.all_to_all(copies, "blk", 0, 0, tiled=True)
    mine_swapped = lax.ppermute(mine, "core", swap)
    spread = jnp.broadcast_to(mine[None], (across, down, 2 * rows, head_size))
    all_mine = lax.all_to_all(spread, "x", 0, 0, tiled=True)
    all_mine = all_mine.reshape(across * down, 2 * rows, head_size)
    all_swapped = lax.ppermute(all_mine, "core", swap)
    state = attend(info(core, x[None], own_kinds), q, mine, None, False, heads)
    state = attend(info(1 - core, x[None], own_kinds), q, mine_swapped, state, False, heads)
    state = attend(info(core, column, other_kinds), q, all_mine, state, False, heads)
    out = attend(info(1 - core, column, other_kinds), q, all_swapped, state, True, heads)
    return out.reshape(rows, heads, head_size)


def solution(mesh):
    blk, uly, tp = mesh.devices.shape
    fine = Mesh(mesh.devices.reshape(blk, uly // 2, 2, tp), ("blk", "x", "core", "tp"))
    spec = P(("blk", "x", "core"), "tp", None)
    return jax.shard_map(
        local, mesh=fine, in_specs=(spec, spec, spec, P()), out_specs=spec, check_vma=False
    )
```

```python
import math

import jax
import jax.numpy as jnp
from jax import lax
from jax.experimental import pallas as pl
from jax.experimental.pallas import tpu as pltpu
from jax.sharding import Mesh, PartitionSpec as P

LOG2E = 1.4426950408889634
MASKED = -1.5e38
START = -1.0e30
FAR = 1 << 20
COLUMNS = 1024
VMEM_BYTES = 40 * 1024 * 1024
VM = pl.BlockSpec(memory_space=pltpu.VMEM)
SM = pl.BlockSpec(memory_space=pltpu.SMEM)
PARAMS = pltpu.CompilerParams(vmem_limit_bytes=VMEM_BYTES)


def split(x):
    high = x.astype(jnp.bfloat16)
    return high, x - high.astype(jnp.float32)


def prepare_kernel(q_ref, other_ref, t_ref):
    total, head_size = q_ref.shape
    for i, ref in enumerate((q_ref, other_ref)):
        scaled = ref[...].astype(jnp.float32).T * (LOG2E / math.sqrt(head_size))
        high, rest = split(scaled)
        t_ref[:head_size, i * total : (i + 1) * total] = high
        t_ref[head_size:, i * total : (i + 1) * total] = rest.astype(jnp.bfloat16)


def prepare(q, other):
    return pl.pallas_call(
        prepare_kernel,
        out_shape=jax.ShapeDtypeStruct((2 * q.shape[1], 2 * q.shape[0]), q.dtype),
        in_specs=[VM, VM],
        out_specs=VM,
        compiler_params=PARAMS,
    )(q, other)


def attend_kernel(shifts, down, first, last, heads, order, q_ref, *refs):
    pieces, refs = refs[: len(shifts)], refs[len(shifts) :]
    if not first:
        m_in, l_in, a_in, *refs = refs
    if last:
        m_out, l_out, a_out, p_out, m_ref, l_ref, a_ref, kv_ref, base = refs
    else:
        m_ref, l_ref, a_ref, kv_ref, base = refs
    if first:
        m_ref[...] = jnp.full(m_ref.shape, START, jnp.float32)
        l_ref[...] = jnp.zeros(l_ref.shape, jnp.float32)
        a_ref[...] = jnp.zeros(a_ref.shape, jnp.float32)
    else:
        m_ref[...] = m_in[...]
        l_ref[...] = l_in[...]
        a_ref[...] = a_in[...]
    depth, total = a_ref.shape
    mine = total // 2
    across, both_rows, _ = pieces[0].shape
    rows = both_rows // 2
    count = across * len(shifts)
    per_span = across // 2
    blk, x, core = lax.axis_index("blk"), lax.axis_index("x"), lax.axis_index("core")
    own_span = order[2 * blk + x // per_span]
    place = (x % per_span) * both_rows

    for i in range(count):
        base[i] = FAR
    free = jnp.int32(0)
    for kind in (1, 2):
        for piece, shift in zip(pieces, shifts):
            row = lax.rem(blk + (down - shift), down)
            for column in range(across):
                here = order[2 * row + column // per_span]
                start = (column % per_span) * both_rows + core * rows
                chosen = here < own_span if kind == 1 else here == own_span
                if kind == 2 and shift != 0:
                    continue

                @pl.when(chosen)
                def _():
                    kv_ref[pl.ds(free, 1)] = piece[column : column + 1]
                    base[free] = -FAR if kind == 1 else start

                free = free + chosen.astype(jnp.int32)
        if kind == 1:
            visible = free

    def fold(group, masked):
        blocks = [kv_ref[i] for i in range(group)]
        k = jnp.concatenate([b[:rows] for b in blocks], axis=0)
        v = jnp.concatenate([b[rows:] for b in blocks], axis=0)
        k = jnp.concatenate([k, k], axis=1)
        parts = range(0, total, COLUMNS)
        scores = [
            jnp.dot(k, q_ref[:, c : c + COLUMNS], preferred_element_type=jnp.float32) for c in parts
        ]
        for c, s in zip(parts, scores):
            at = pl.ds(c, COLUMNS)
            if masked:
                shape = (rows, COLUMNS)
                lane = lax.broadcasted_iota(jnp.int32, shape, 1) + c % mine
                query_core = core if c < mine else 1 - core
                gap = place + query_core * rows + lane // heads - lax.broadcasted_iota(jnp.int32, shape, 0)
                s = jnp.concatenate(
                    [
                        jnp.where(gap >= base[i], s[i * rows : (i + 1) * rows], MASKED)
                        for i in range(group)
                    ],
                    axis=0,
                )
            m_old = m_ref[:, at]
            m_new = jnp.maximum(m_old, jnp.max(s, axis=0, keepdims=True))
            alpha = jnp.exp2(m_old - m_new)
            p = jnp.exp2(s - m_new)
            m_ref[:, at] = m_new
            l_ref[:, at] = l_ref[:, at] * alpha + jnp.sum(p, axis=0, keepdims=True)
            a_ref[:, at] = a_ref[:, at] * alpha + lax.dot_general(
                v,
                p.astype(jnp.bfloat16),
                (((0,), (0,)), ((), ())),
                preferred_element_type=jnp.float32,
            )

    @pl.when(visible == count)
    def _():
        fold(count, False)

    if count > 4:

        @pl.when((visible < count) & (free > 4))
        def _():
            for i in range(4, count):

                @pl.when(i >= free)
                def _():
                    kv_ref[i] = jnp.zeros(kv_ref.shape[1:], kv_ref.dtype)

            fold(count, True)

    @pl.when((visible < count) & (free > 0) & (free <= 4))
    def _():
        for i in range(1, 4):

            @pl.when(i >= free)
            def _():
                kv_ref[i] = jnp.zeros(kv_ref.shape[1:], kv_ref.dtype)

        fold(4, True)

    if last:
        m_out[...] = m_ref[:, :mine]
        l_out[...] = l_ref[:, :mine]
        a_out[...] = a_ref[:, :mine]
        l = l_ref[:, mine:]
        some = l > 0.0
        p_out[:depth, :] = (a_ref[:, mine:] / jnp.where(some, l, 1.0)).astype(jnp.bfloat16)
        level = jnp.where(some, m_ref[:, mine:] + jnp.log(jnp.where(some, l, 1.0)) * LOG2E, START)
        high, rest = split(level)
        mid, rest = split(rest)
        line = lax.broadcasted_iota(jnp.int32, (p_out.shape[0] - depth, mine), 0)
        packed = jnp.where(
            line == 0,
            high.astype(jnp.float32),
            jnp.where(line == 1, mid.astype(jnp.float32), jnp.where(line == 2, rest, 0.0)),
        )
        p_out[depth:, :] = packed.astype(jnp.bfloat16)


def attend(order, q, pieces, shifts, state, last, heads, down):
    total = q.shape[1]
    across, both_rows, head_size = pieces[0].shape
    count = across * len(pieces)
    first = state is None
    args = [order, q] + list(pieces) + ([] if first else list(state))

    def shapes(n):
        stat = jax.ShapeDtypeStruct((1, n), jnp.float32)
        return [stat, stat, jax.ShapeDtypeStruct((head_size, n), jnp.float32)]

    extra = [
        pltpu.VMEM((count, both_rows, head_size), jnp.bfloat16),
        pltpu.SMEM((count + 1,), jnp.int32),
    ]
    if last:
        packet = jax.ShapeDtypeStruct((head_size + 16, total // 2), jnp.bfloat16)
        out_shape = shapes(total // 2) + [packet]
        scratch = [pltpu.VMEM(s.shape, s.dtype) for s in shapes(total)] + extra
    else:
        out_shape, scratch = shapes(total), extra

    def body(*refs):
        attend_kernel(shifts, down, first, last, heads, *refs)

    keys = count * both_rows // 2
    return pl.pallas_call(
        body,
        out_shape=out_shape,
        in_specs=[SM] + [VM] * (len(args) - 1),
        out_specs=[VM] * len(out_shape),
        scratch_shapes=scratch,
        compiler_params=PARAMS,
        cost_estimate=pl.CostEstimate(
            flops=4 * total * keys * head_size,
            bytes_accessed=4 * keys * head_size + 2 * total * head_size,
            transcendentals=total * keys,
        ),
    )(*args)


def combine_kernel(m_ref, l_ref, a_ref, p_ref, out_ref):
    depth = a_ref.shape[0]
    level = (
        p_ref[depth : depth + 1].astype(jnp.float32)
        + p_ref[depth + 1 : depth + 2].astype(jnp.float32)
        + p_ref[depth + 2 : depth + 3].astype(jnp.float32)
    )
    top = jnp.maximum(m_ref[...], level)
    here, there = jnp.exp2(m_ref[...] - top), jnp.exp2(level - top)
    whole = 1.0 / (l_ref[...] * here + there)
    mixed = a_ref[...] * (here * whole) + p_ref[:depth].astype(jnp.float32) * (there * whole)
    out_ref[...] = mixed.T.astype(jnp.bfloat16)


def combine(m, l, a, packet):
    return pl.pallas_call(
        combine_kernel,
        out_shape=jax.ShapeDtypeStruct(a.shape[::-1], jnp.bfloat16),
        in_specs=[VM] * 4,
        out_specs=VM,
        compiler_params=PARAMS,
    )(m, l, a, packet)


def local(queries, keys, values, span_order):
    rows, heads, head_size = queries.shape
    down, across = lax.axis_size("blk"), lax.axis_size("x")
    swap = [(0, 1), (1, 0)]
    own = queries.reshape(rows * heads, head_size)
    other = lax.ppermute(own, "core", swap)
    kv = jnp.concatenate([keys.reshape(rows, head_size), values.reshape(rows, head_size)], axis=0)
    copies = jnp.broadcast_to(kv[None], (across, 2 * rows, head_size))
    row = lax.all_to_all(copies, "x", 0, 0, tiled=True)
    up = [(i, (i + 1) % down) for i in range(down)]
    back = [(i, (i - 1) % down) for i in range(down)]
    q = prepare(own, other)
    state = attend(span_order, q, [row], [0], None, False, heads, down)
    rising = falling = row
    for hop in range(1, down // 2):
        rising = lax.ppermute(rising, "blk", up)
        falling = lax.ppermute(falling, "blk", back)
        state = attend(
            span_order, q, [rising, falling], [hop, down - hop], state, False, heads, down
        )
    rising = lax.ppermute(rising, "blk", up)
    m, l, a, packet = attend(span_order, q, [rising], [down // 2], state, True, heads, down)
    packet = lax.ppermute(packet, "core", swap)
    return combine(m, l, a, packet).reshape(rows, heads, head_size)


def solution(mesh):
    blk, uly, tp = mesh.devices.shape
    fine = Mesh(mesh.devices.reshape(blk, uly // 2, 2, tp), ("blk", "x", "core", "tp"))
    spec = P(("blk", "x", "core"), "tp", None)
    return jax.shard_map(
        local, mesh=fine, in_specs=(spec, spec, spec, P()), out_specs=spec, check_vma=False
    )
```

```python
import math

import jax
import jax.numpy as jnp
from jax import lax
from jax.experimental import pallas as pl
from jax.experimental.pallas import tpu as pltpu
from jax.sharding import Mesh, PartitionSpec as P

LOG2E = 1.4426950408889634
MASKED = -1.5e38
START = -1.0e30
FAR = 1 << 20
COLUMNS = 512
AHEAD = 1
ROOM = 100.0
VMEM_BYTES = 40 * 1024 * 1024
VM = pl.BlockSpec(memory_space=pltpu.VMEM)
SM = pl.BlockSpec(memory_space=pltpu.SMEM)
PARAMS = pltpu.CompilerParams(vmem_limit_bytes=VMEM_BYTES)


def split(x):
    high = x.astype(jnp.bfloat16)
    return high, x - high.astype(jnp.float32)


def prepare_kernel(q_ref, other_ref, t_ref):
    total, head_size = q_ref.shape
    for i, ref in enumerate((q_ref, other_ref)):
        scaled = ref[...].astype(jnp.float32).T * (LOG2E / math.sqrt(head_size))
        high, rest = split(scaled)
        t_ref[:head_size, i * total : (i + 1) * total] = high
        t_ref[head_size:, i * total : (i + 1) * total] = rest.astype(jnp.bfloat16)


def prepare(q, other):
    return pl.pallas_call(
        prepare_kernel,
        out_shape=jax.ShapeDtypeStruct((2 * q.shape[1], 2 * q.shape[0]), q.dtype),
        in_specs=[VM, VM],
        out_specs=VM,
        compiler_params=PARAMS,
    )(q, other)


def attend_kernel(shifts, down, first, last, heads, order, q_ref, *refs):
    pieces, refs = refs[: len(shifts)], refs[len(shifts) :]
    if not first:
        m_in, l_in, a_in, *refs = refs
    if last:
        m_out, l_out, a_out, p_out, m_ref, l_ref, a_ref, kv_ref, base = refs
    else:
        m_ref, l_ref, a_ref, kv_ref, base = refs
    depth, total = a_ref.shape
    mine = total // 2
    across, both_rows, _ = pieces[0].shape
    rows = both_rows // 2
    count = across * len(shifts)
    per_span = across // 2
    blk, x, core = lax.axis_index("blk"), lax.axis_index("x"), lax.axis_index("core")
    own_span = order[2 * blk + x // per_span]
    place = (x % per_span) * both_rows

    for i in range(count):
        base[i] = FAR
    free = jnp.int32(0)
    for kind in (1, 2):
        for piece, shift in zip(pieces, shifts):
            if kind == 2 and shift != 0:
                continue
            row = lax.rem(blk + (down - shift), down)
            for column in range(across):
                here = order[2 * row + column // per_span]
                start = (column % per_span) * both_rows + core * rows
                chosen = here < own_span if kind == 1 else here == own_span

                @pl.when(chosen)
                def _():
                    kv_ref[pl.ds(free, 1)] = piece[column : column + 1]
                    base[free] = -FAR if kind == 1 else start

                free = free + chosen.astype(jnp.int32)
    for i in range(count):

        @pl.when(i >= free)
        def _():
            kv_ref[i] = jnp.zeros(kv_ref.shape[1:], kv_ref.dtype)

    def hide(s, c, group):
        if first:
            shape = (rows, COLUMNS)
            lane = lax.broadcasted_iota(jnp.int32, shape, 1) + c % mine
            query_core = core if c < mine else 1 - core
            gap = place + query_core * rows + lane // heads - lax.broadcasted_iota(jnp.int32, shape, 0)
            seen = [gap >= base[i] for i in range(group)]
        else:
            seen = [i < free for i in range(group)]
        return jnp.concatenate(
            [jnp.where(seen[i], s[i * rows : (i + 1) * rows], MASKED) for i in range(group)], axis=0
        )

    def fold(group, partial, exact):
        blocks = [kv_ref[i] for i in range(group)]
        k = jnp.concatenate([b[:rows] for b in blocks], axis=0)
        v = jnp.concatenate([b[rows:] for b in blocks], axis=0)
        k = jnp.concatenate([k, k], axis=1)
        parts = list(range(0, total, COLUMNS))
        worst = jnp.zeros((1, COLUMNS), jnp.float32)

        def score(c):
            return jnp.dot(k, q_ref[:, c : c + COLUMNS], preferred_element_type=jnp.float32)

        ahead = [score(c) for c in parts[:AHEAD]]
        for i, c in enumerate(parts):
            if i + AHEAD < len(parts):
                ahead.append(score(parts[i + AHEAD]))
            raw = ahead[i]
            at = pl.ds(c, COLUMNS)
            s = hide(raw, c, group) if partial else raw
            top = jnp.max(s, axis=0, keepdims=True)
            if first:
                m = jnp.where(top > 0.5 * MASKED, top, jnp.max(raw, axis=0, keepdims=True))
            elif exact:
                l_old = l_in[:, at]
                m_old = jnp.where(l_old > 0.0, m_in[:, at], START)
                m = jnp.maximum(m_old, top)
                alpha = jnp.exp2(m_old - m)
            else:
                m = m_in[:, at]
                low = (l_in[:, at] == 0.0) & (top > 0.5 * MASKED) & (top < m - ROOM)
                worst = jnp.maximum(worst, jnp.where((top > m + ROOM) | low, 1.0, 0.0))
            p = jnp.exp2(s - m)
            l_new = jnp.sum(p, axis=0, keepdims=True)
            a_new = lax.dot_general(
                v,
                p.astype(jnp.bfloat16),
                (((0,), (0,)), ((), ())),
                preferred_element_type=jnp.float32,
            )
            m_ref[:, at] = m
            if first:
                l_ref[:, at] = l_new
                a_ref[:, at] = a_new
            elif exact:
                l_ref[:, at] = l_old * alpha + l_new
                a_ref[:, at] = a_in[:, at] * alpha + a_new
            else:
                l_ref[:, at] = l_in[:, at] + l_new
                a_ref[:, at] = a_in[:, at] + a_new
        return worst

    if first:
        fold(count, True, True)
    else:
        base[count] = 0

        def attempt(group, partial):
            base[count] = (jnp.max(fold(group, partial, False)) > 0.0).astype(jnp.int32)

        @pl.when(free == 0)
        def _():
            m_ref[...] = m_in[...]
            l_ref[...] = l_in[...]
            a_ref[...] = a_in[...]

        pl.when(free == count)(lambda: attempt(count, False))
        if count > 4:
            pl.when((free > 4) & (free < count))(lambda: attempt(count, True))
            pl.when((free > 0) & (free <= 4))(lambda: attempt(4, True))
        else:
            pl.when((free > 0) & (free < count))(lambda: attempt(count, True))

        @pl.when(base[count] > 0)
        def _():
            fold(count, True, True)

    if last:
        m_out[...] = m_ref[:, :mine]
        l_out[...] = l_ref[:, :mine]
        a_out[...] = a_ref[:, :mine]
        l = l_ref[:, mine:]
        some = l > 0.0
        p_out[:depth, :] = (a_ref[:, mine:] / jnp.where(some, l, 1.0)).astype(jnp.bfloat16)
        level = jnp.where(some, m_ref[:, mine:] + jnp.log(jnp.where(some, l, 1.0)) * LOG2E, START)
        high, rest = split(level)
        mid, rest = split(rest)
        line = lax.broadcasted_iota(jnp.int32, (p_out.shape[0] - depth, mine), 0)
        packed = jnp.where(
            line == 0,
            high.astype(jnp.float32),
            jnp.where(line == 1, mid.astype(jnp.float32), jnp.where(line == 2, rest, 0.0)),
        )
        p_out[depth:, :] = packed.astype(jnp.bfloat16)


def attend(order, q, pieces, shifts, state, last, heads, down):
    total = q.shape[1]
    across, both_rows, head_size = pieces[0].shape
    count = across * len(pieces)
    first = state is None
    args = [order, q] + list(pieces) + ([] if first else list(state))

    def shapes(n):
        stat = jax.ShapeDtypeStruct((1, n), jnp.float32)
        return [stat, stat, jax.ShapeDtypeStruct((head_size, n), jnp.float32)]

    extra = [
        pltpu.VMEM((count, both_rows, head_size), jnp.bfloat16),
        pltpu.SMEM((count + 1,), jnp.int32),
    ]
    if last:
        packet = jax.ShapeDtypeStruct((head_size + 16, total // 2), jnp.bfloat16)
        out_shape = shapes(total // 2) + [packet]
        scratch = [pltpu.VMEM(s.shape, s.dtype) for s in shapes(total)] + extra
    else:
        out_shape, scratch = shapes(total), extra

    def body(*refs):
        attend_kernel(shifts, down, first, last, heads, *refs)

    keys = count * both_rows // 2
    return pl.pallas_call(
        body,
        out_shape=out_shape,
        in_specs=[SM] + [VM] * (len(args) - 1),
        out_specs=[VM] * len(out_shape),
        scratch_shapes=scratch,
        compiler_params=PARAMS,
        cost_estimate=pl.CostEstimate(
            flops=4 * total * keys * head_size,
            bytes_accessed=4 * keys * head_size + 2 * total * head_size,
            transcendentals=total * keys,
        ),
    )(*args)


def combine_kernel(m_ref, l_ref, a_ref, p_ref, out_ref):
    depth = a_ref.shape[0]
    level = (
        p_ref[depth : depth + 1].astype(jnp.float32)
        + p_ref[depth + 1 : depth + 2].astype(jnp.float32)
        + p_ref[depth + 2 : depth + 3].astype(jnp.float32)
    )
    top = jnp.maximum(m_ref[...], level)
    here, there = jnp.exp2(m_ref[...] - top), jnp.exp2(level - top)
    whole = 1.0 / (l_ref[...] * here + there)
    mixed = a_ref[...] * (here * whole) + p_ref[:depth].astype(jnp.float32) * (there * whole)
    out_ref[...] = mixed.T.astype(jnp.bfloat16)


def combine(m, l, a, packet):
    return pl.pallas_call(
        combine_kernel,
        out_shape=jax.ShapeDtypeStruct(a.shape[::-1], jnp.bfloat16),
        in_specs=[VM] * 4,
        out_specs=VM,
        compiler_params=PARAMS,
    )(m, l, a, packet)


def local(queries, keys, values, span_order):
    rows, heads, head_size = queries.shape
    down, across = lax.axis_size("blk"), lax.axis_size("x")
    swap = [(0, 1), (1, 0)]
    own = queries.reshape(rows * heads, head_size)
    other = lax.ppermute(own, "core", swap)
    kv = jnp.concatenate([keys.reshape(rows, head_size), values.reshape(rows, head_size)], axis=0)
    copies = jnp.broadcast_to(kv[None], (across, 2 * rows, head_size))
    row = lax.all_to_all(copies, "x", 0, 0, tiled=True)
    up = [(i, (i + 1) % down) for i in range(down)]
    back = [(i, (i - 1) % down) for i in range(down)]
    q = prepare(own, other)
    state = attend(span_order, q, [row], [0], None, False, heads, down)
    rising = falling = row
    for hop in range(1, down // 2):
        rising = lax.ppermute(rising, "blk", up)
        falling = lax.ppermute(falling, "blk", back)
        if hop <= 2:
            rising, state = lax.optimization_barrier((rising, state))
        state = attend(
            span_order, q, [rising, falling], [hop, down - hop], state, False, heads, down
        )
    rising = lax.ppermute(rising, "blk", up)
    m, l, a, packet = attend(span_order, q, [rising], [down // 2], state, True, heads, down)
    packet = lax.ppermute(packet, "core", swap)
    return combine(m, l, a, packet).reshape(rows, heads, head_size)


def solution(mesh):
    blk, uly, tp = mesh.devices.shape
    fine = Mesh(mesh.devices.reshape(blk, uly // 2, 2, tp), ("blk", "x", "core", "tp"))
    spec = P(("blk", "x", "core"), "tp", None)
    return jax.shard_map(
        local, mesh=fine, in_specs=(spec, spec, spec, P()), out_specs=spec, check_vma=False
    )
```

```python
import math

import jax
import jax.numpy as jnp
from jax import lax
from jax.experimental import pallas as pl
from jax.experimental.pallas import tpu as pltpu
from jax.sharding import Mesh, PartitionSpec as P

LOG2E = 1.4426950408889634
MASKED = -1.5e38
START = -1.0e30
FAR = 1 << 20
COLUMNS = 512
AHEAD = 1
ROOM = 100.0
VMEM_BYTES = 40 * 1024 * 1024
VM = pl.BlockSpec(memory_space=pltpu.VMEM)
SM = pl.BlockSpec(memory_space=pltpu.SMEM)
PARAMS = pltpu.CompilerParams(vmem_limit_bytes=VMEM_BYTES)


def split(x):
    high = x.astype(jnp.bfloat16)
    return high, x - high.astype(jnp.float32)


def prepare_kernel(q_ref, other_ref, t_ref):
    total, head_size = q_ref.shape
    for i, ref in enumerate((q_ref, other_ref)):
        scaled = ref[...].astype(jnp.float32).T * (LOG2E / math.sqrt(head_size))
        high, rest = split(scaled)
        t_ref[:head_size, i * total : (i + 1) * total] = high
        t_ref[head_size:, i * total : (i + 1) * total] = rest.astype(jnp.bfloat16)


def prepare(q, other):
    return pl.pallas_call(
        prepare_kernel,
        out_shape=jax.ShapeDtypeStruct((2 * q.shape[1], 2 * q.shape[0]), q.dtype),
        in_specs=[VM, VM],
        out_specs=VM,
        compiler_params=PARAMS,
    )(q, other)


def attend_kernel(shifts, down, columns, state_in, theirs, heads, order, q_ref, *refs):
    pieces, refs = refs[: len(shifts)], refs[len(shifts) :]
    first = not state_in
    if not first:
        m_in, l_in, a_in, *refs = refs
    if theirs:
        p_out, *refs = refs
    m_ref, l_ref, a_ref, kv_ref, base = refs
    low_column, high_column = columns
    depth, total = a_ref.shape[0], q_ref.shape[1]
    mine = total // 2
    across, both_rows, _ = pieces[0].shape
    rows = both_rows // 2
    count = across * len(shifts)
    per_span = across // 2
    blk, x, core = lax.axis_index("blk"), lax.axis_index("x"), lax.axis_index("core")
    own_span = order[2 * blk + x // per_span]
    place = (x % per_span) * both_rows

    for i in range(count):
        base[i] = FAR
    free = jnp.int32(0)
    for kind in (1, 2):
        for piece, shift in zip(pieces, shifts):
            if kind == 2 and shift != 0:
                continue
            row = lax.rem(blk + (down - shift), down)
            for column in range(across):
                here = order[2 * row + column // per_span]
                start = (column % per_span) * both_rows + core * rows
                chosen = here < own_span if kind == 1 else here == own_span

                @pl.when(chosen)
                def _():
                    kv_ref[pl.ds(free, 1)] = piece[column : column + 1]
                    base[free] = -FAR if kind == 1 else start

                free = free + chosen.astype(jnp.int32)
    for i in range(count):

        @pl.when(i >= free)
        def _():
            kv_ref[i] = jnp.zeros(kv_ref.shape[1:], kv_ref.dtype)

    def hide(s, c, group):
        if first:
            shape = (rows, COLUMNS)
            lane = lax.broadcasted_iota(jnp.int32, shape, 1) + c % mine
            query_core = core if c < mine else 1 - core
            gap = place + query_core * rows + lane // heads - lax.broadcasted_iota(jnp.int32, shape, 0)
            seen = [gap >= base[i] for i in range(group)]
        else:
            seen = [i < free for i in range(group)]
        return jnp.concatenate(
            [jnp.where(seen[i], s[i * rows : (i + 1) * rows], MASKED) for i in range(group)], axis=0
        )

    def fold(group, partial, exact):
        blocks = [kv_ref[i] for i in range(group)]
        k = jnp.concatenate([b[:rows] for b in blocks], axis=0)
        v = jnp.concatenate([b[rows:] for b in blocks], axis=0)
        k = jnp.concatenate([k, k], axis=1)
        parts = list(range(low_column, high_column, COLUMNS))
        worst = jnp.zeros((1, COLUMNS), jnp.float32)

        def score(c):
            return jnp.dot(k, q_ref[:, c : c + COLUMNS], preferred_element_type=jnp.float32)

        ahead = [score(c) for c in parts[:AHEAD]]
        for i, c in enumerate(parts):
            if i + AHEAD < len(parts):
                ahead.append(score(parts[i + AHEAD]))
            raw = ahead[i]
            at, to = pl.ds(c, COLUMNS), pl.ds(c - low_column, COLUMNS)
            s = hide(raw, c, group) if partial else raw
            top = jnp.max(s, axis=0, keepdims=True)
            if first:
                m = jnp.where(top > 0.5 * MASKED, top, jnp.max(raw, axis=0, keepdims=True))
            elif exact:
                l_old = l_in[:, at]
                m_old = jnp.where(l_old > 0.0, m_in[:, at], START)
                m = jnp.maximum(m_old, top)
                alpha = jnp.exp2(m_old - m)
            else:
                m = m_in[:, at]
                low = (l_in[:, at] == 0.0) & (top > 0.5 * MASKED) & (top < m - ROOM)
                worst = jnp.maximum(worst, jnp.where((top > m + ROOM) | low, 1.0, 0.0))
            p = jnp.exp2(s - m)
            l_new = jnp.sum(p, axis=0, keepdims=True)
            a_new = lax.dot_general(
                v,
                p.astype(jnp.bfloat16),
                (((0,), (0,)), ((), ())),
                preferred_element_type=jnp.float32,
            )
            m_ref[:, to] = m
            if first:
                l_ref[:, to] = l_new
                a_ref[:, to] = a_new
            elif exact:
                l_ref[:, to] = l_old * alpha + l_new
                a_ref[:, to] = a_in[:, at] * alpha + a_new
            else:
                l_ref[:, to] = l_in[:, at] + l_new
                a_ref[:, to] = a_in[:, at] + a_new
        return worst

    if first:
        fold(count, True, True)
    else:
        base[count] = 0

        def attempt(group, partial):
            base[count] = (jnp.max(fold(group, partial, False)) > 0.0).astype(jnp.int32)

        @pl.when(free == 0)
        def _():
            m_ref[...] = m_in[:, low_column:high_column]
            l_ref[...] = l_in[:, low_column:high_column]
            a_ref[...] = a_in[:, low_column:high_column]

        pl.when(free == count)(lambda: attempt(count, False))
        if count > 4:
            pl.when((free > 4) & (free < count))(lambda: attempt(count, True))
            pl.when((free > 0) & (free <= 4))(lambda: attempt(4, True))
        else:
            pl.when((free > 0) & (free < count))(lambda: attempt(count, True))

        @pl.when(base[count] > 0)
        def _():
            fold(count, True, True)

    if theirs:
        l = l_ref[...]
        some = l > 0.0
        p_out[:depth, :] = (a_ref[...] / jnp.where(some, l, 1.0)).astype(jnp.bfloat16)
        level = jnp.where(some, m_ref[...] + jnp.log(jnp.where(some, l, 1.0)) * LOG2E, START)
        high, rest = split(level)
        mid, rest = split(rest)
        line = lax.broadcasted_iota(jnp.int32, (p_out.shape[0] - depth, mine), 0)
        packed = jnp.where(
            line == 0,
            high.astype(jnp.float32),
            jnp.where(line == 1, mid.astype(jnp.float32), jnp.where(line == 2, rest, 0.0)),
        )
        p_out[depth:, :] = packed.astype(jnp.bfloat16)


def attend(order, q, pieces, shifts, state, heads, down, columns=None, theirs=False):
    total = q.shape[1]
    columns = columns or (0, total)
    width = columns[1] - columns[0]
    across, both_rows, head_size = pieces[0].shape
    count = across * len(pieces)
    args = [order, q] + list(pieces) + list(state)
    stat = jax.ShapeDtypeStruct((1, width), jnp.float32)
    out_shape = [stat, stat, jax.ShapeDtypeStruct((head_size, width), jnp.float32)]
    scratch = [
        pltpu.VMEM((count, both_rows, head_size), jnp.bfloat16),
        pltpu.SMEM((count + 1,), jnp.int32),
    ]
    if theirs:
        scratch = [pltpu.VMEM(s.shape, s.dtype) for s in out_shape] + scratch
        out_shape = [jax.ShapeDtypeStruct((head_size + 16, width), jnp.bfloat16)]

    def body(*refs):
        attend_kernel(shifts, down, columns, len(state) > 0, theirs, heads, *refs)

    keys = count * both_rows // 2
    return pl.pallas_call(
        body,
        out_shape=out_shape,
        in_specs=[SM] + [VM] * (len(args) - 1),
        out_specs=[VM] * len(out_shape),
        scratch_shapes=scratch,
        compiler_params=PARAMS,
        cost_estimate=pl.CostEstimate(
            flops=4 * width * keys * head_size,
            bytes_accessed=4 * keys * head_size + 2 * width * head_size,
            transcendentals=width * keys,
        ),
    )(*args)


def combine_kernel(m_ref, l_ref, a_ref, p_ref, out_ref):
    depth = a_ref.shape[0]
    level = (
        p_ref[depth : depth + 1].astype(jnp.float32)
        + p_ref[depth + 1 : depth + 2].astype(jnp.float32)
        + p_ref[depth + 2 : depth + 3].astype(jnp.float32)
    )
    top = jnp.maximum(m_ref[...], level)
    here, there = jnp.exp2(m_ref[...] - top), jnp.exp2(level - top)
    whole = 1.0 / (l_ref[...] * here + there)
    mixed = a_ref[...] * (here * whole) + p_ref[:depth].astype(jnp.float32) * (there * whole)
    out_ref[...] = mixed.T.astype(jnp.bfloat16)


def combine(m, l, a, packet):
    return pl.pallas_call(
        combine_kernel,
        out_shape=jax.ShapeDtypeStruct(a.shape[::-1], jnp.bfloat16),
        in_specs=[VM] * 4,
        out_specs=VM,
        compiler_params=PARAMS,
    )(m, l, a, packet)


def local(queries, keys, values, span_order):
    rows, heads, head_size = queries.shape
    down, across = lax.axis_size("blk"), lax.axis_size("x")
    swap = [(0, 1), (1, 0)]
    own = queries.reshape(rows * heads, head_size)
    other = lax.ppermute(own, "core", swap)
    wide = (across, rows, head_size)
    k = jnp.broadcast_to(keys.reshape(1, rows, head_size), wide)
    v = jnp.broadcast_to(values.reshape(1, rows, head_size), wide)
    spread = jnp.concatenate([k, v], axis=1)
    row = lax.all_to_all(spread, "x", 0, 0, tiled=True)
    up = [(i, (i + 1) % down) for i in range(down)]
    back = [(i, (i - 1) % down) for i in range(down)]
    q = prepare(own, other)
    state = attend(span_order, q, [row], [0], (), heads, down)
    rising = falling = row
    for hop in range(1, down // 2):
        rising = lax.ppermute(rising, "blk", up)
        falling = lax.ppermute(falling, "blk", back)
        if hop <= 2:
            rising, state = lax.optimization_barrier((rising, state))
        state = attend(span_order, q, [rising, falling], [hop, down - hop], state, heads, down)
    farthest = lax.ppermute(rising, "blk", up)
    mine = q.shape[1] // 2
    half, other_half = (0, mine), (mine, 2 * mine)
    (packet,) = attend(
        span_order, q, [farthest], [down // 2], state, heads, down, other_half, True
    )
    packet, state = lax.optimization_barrier((packet, state))
    theirs = lax.ppermute(packet, "core", swap)
    m, l, a = attend(span_order, q, [farthest], [down // 2], state, heads, down, half)
    return combine(m, l, a, theirs).reshape(rows, heads, head_size)


def solution(mesh):
    blk, uly, tp = mesh.devices.shape
    fine = Mesh(mesh.devices.reshape(blk, uly // 2, 2, tp), ("blk", "x", "core", "tp"))
    spec = P(("blk", "x", "core"), "tp", None)
    return jax.shard_map(
        local, mesh=fine, in_specs=(spec, spec, spec, P()), out_specs=spec, check_vma=False
    )
```

```python
import math

import jax
import jax.numpy as jnp
from jax import lax
from jax.experimental import pallas as pl
from jax.experimental.pallas import tpu as pltpu
from jax.sharding import Mesh, PartitionSpec as P

LOG2E = 1.4426950408889634
MASKED = -1.5e38
START = -1.0e30
FAR = 1 << 20
COLUMNS = 512
AHEAD = 1
ROOM = 100.0
VMEM_BYTES = 40 * 1024 * 1024
VM = pl.BlockSpec(memory_space=pltpu.VMEM)
SM = pl.BlockSpec(memory_space=pltpu.SMEM)
PARAMS = pltpu.CompilerParams(vmem_limit_bytes=VMEM_BYTES)


def split(x):
    high = x.astype(jnp.bfloat16)
    return high, x - high.astype(jnp.float32)


def prepare_kernel(q_ref, other_ref, t_ref):
    total, head_size = q_ref.shape
    for i, ref in enumerate((q_ref, other_ref)):
        scaled = ref[...].astype(jnp.float32).T * (LOG2E / math.sqrt(head_size))
        high, rest = split(scaled)
        t_ref[:head_size, i * total : (i + 1) * total] = high
        t_ref[head_size:, i * total : (i + 1) * total] = rest.astype(jnp.bfloat16)


def prepare(q, other):
    return pl.pallas_call(
        prepare_kernel,
        out_shape=jax.ShapeDtypeStruct((2 * q.shape[1], 2 * q.shape[0]), q.dtype),
        in_specs=[VM, VM],
        out_specs=VM,
        compiler_params=PARAMS,
    )(q, other)


def attend_kernel(shifts, down, columns, state_in, theirs, heads, order, q_ref, *refs):
    pieces, refs = refs[: len(shifts)], refs[len(shifts) :]
    first = not state_in
    if not first:
        m_in, l_in, a_in, *refs = refs
    if theirs:
        p_out, *refs = refs
    m_ref, l_ref, a_ref, kv_ref, base = refs
    low_column, high_column = columns
    depth, total = a_ref.shape[0], q_ref.shape[1]
    mine = total // 2
    across, both_rows, _ = pieces[0].shape
    rows = both_rows // 2
    count = across * len(shifts)
    per_span = across // 2
    blk, x, core = lax.axis_index("blk"), lax.axis_index("x"), lax.axis_index("core")
    own_span = order[2 * blk + x // per_span]
    place = (x % per_span) * both_rows

    for i in range(count):
        base[i] = FAR
    free = jnp.int32(0)
    for kind in (1, 2):
        for piece, shift in zip(pieces, shifts):
            if kind == 2 and shift != 0:
                continue
            row = lax.rem(blk + (down - shift), down)
            for column in range(across):
                here = order[2 * row + column // per_span]
                start = (column % per_span) * both_rows + core * rows
                chosen = here < own_span if kind == 1 else here == own_span

                @pl.when(chosen)
                def _():
                    kv_ref[pl.ds(free, 1)] = piece[column : column + 1]
                    base[free] = -FAR if kind == 1 else start

                free = free + chosen.astype(jnp.int32)
    for i in range(count):

        @pl.when(i >= free)
        def _():
            kv_ref[i] = jnp.zeros(kv_ref.shape[1:], kv_ref.dtype)

    def hide(s, c, group):
        if first:
            shape = (rows, COLUMNS)
            lane = lax.broadcasted_iota(jnp.int32, shape, 1) + c % mine
            query_core = core if c < mine else 1 - core
            gap = place + query_core * rows + lane // heads - lax.broadcasted_iota(jnp.int32, shape, 0)
            seen = [gap >= base[i] for i in range(group)]
        else:
            seen = [i < free for i in range(group)]
        return jnp.concatenate(
            [jnp.where(seen[i], s[i * rows : (i + 1) * rows], MASKED) for i in range(group)], axis=0
        )

    def fold(group, partial, exact):
        blocks = [kv_ref[i] for i in range(group)]
        k = jnp.concatenate([b[:rows] for b in blocks], axis=0)
        v = jnp.concatenate([b[rows:] for b in blocks], axis=0)
        k = jnp.concatenate([k, k], axis=1)
        parts = list(range(low_column, high_column, COLUMNS))
        worst = jnp.zeros((1, COLUMNS), jnp.float32)

        def score(c):
            return jnp.dot(k, q_ref[:, c : c + COLUMNS], preferred_element_type=jnp.float32)

        ahead = [score(c) for c in parts[:AHEAD]]
        for i, c in enumerate(parts):
            if i + AHEAD < len(parts):
                ahead.append(score(parts[i + AHEAD]))
            raw = ahead[i]
            at, to = pl.ds(c, COLUMNS), pl.ds(c - low_column, COLUMNS)
            s = hide(raw, c, group) if partial else raw
            top = jnp.max(s, axis=0, keepdims=True)
            if first:
                m = jnp.where(top > 0.5 * MASKED, top, jnp.max(raw, axis=0, keepdims=True))
            elif exact:
                l_old = l_in[:, at]
                m_old = jnp.where(l_old > 0.0, m_in[:, at], START)
                m = jnp.maximum(m_old, top)
                alpha = jnp.exp2(m_old - m)
            else:
                m = m_in[:, at]
                low = (l_in[:, at] == 0.0) & (top > 0.5 * MASKED) & (top < m - ROOM)
                worst = jnp.maximum(worst, jnp.where((top > m + ROOM) | low, 1.0, 0.0))
            p = jnp.exp2(s - m)
            l_new = jnp.sum(p, axis=0, keepdims=True)
            a_new = lax.dot_general(
                v,
                p.astype(jnp.bfloat16),
                (((0,), (0,)), ((), ())),
                preferred_element_type=jnp.float32,
            )
            m_ref[:, to] = m
            if first:
                l_ref[:, to] = l_new
                a_ref[:, to] = a_new
            elif exact:
                l_ref[:, to] = l_old * alpha + l_new
                a_ref[:, to] = a_in[:, at] * alpha + a_new
            else:
                l_ref[:, to] = l_in[:, at] + l_new
                a_ref[:, to] = a_in[:, at] + a_new
        return worst

    if first:
        fold(count, True, True)
    else:
        base[count] = 0

        def attempt(group, partial):
            base[count] = (jnp.max(fold(group, partial, False)) > 0.0).astype(jnp.int32)

        @pl.when(free == 0)
        def _():
            m_ref[...] = m_in[:, low_column:high_column]
            l_ref[...] = l_in[:, low_column:high_column]
            a_ref[...] = a_in[:, low_column:high_column]

        pl.when(free == count)(lambda: attempt(count, False))
        if count > 4:
            pl.when((free > 4) & (free < count))(lambda: attempt(count, True))
            pl.when((free > 0) & (free <= 4))(lambda: attempt(4, True))
        else:
            pl.when((free > 0) & (free < count))(lambda: attempt(count, True))

        @pl.when(base[count] > 0)
        def _():
            fold(count, True, True)

    if theirs:
        l = l_ref[...]
        some = l > 0.0
        p_out[:depth, :] = (a_ref[...] / jnp.where(some, l, 1.0)).astype(jnp.bfloat16)
        level = jnp.where(some, m_ref[...] + jnp.log(jnp.where(some, l, 1.0)) * LOG2E, START)
        high, rest = split(level)
        mid, rest = split(rest)
        line = lax.broadcasted_iota(jnp.int32, (p_out.shape[0] - depth, mine), 0)
        packed = jnp.where(
            line == 0,
            high.astype(jnp.float32),
            jnp.where(line == 1, mid.astype(jnp.float32), jnp.where(line == 2, rest, 0.0)),
        )
        p_out[depth:, :] = packed.astype(jnp.bfloat16)


def attend(order, q, pieces, shifts, state, heads, down, columns=None, theirs=False):
    total = q.shape[1]
    columns = columns or (0, total)
    width = columns[1] - columns[0]
    across, both_rows, head_size = pieces[0].shape
    count = across * len(pieces)
    args = [order, q] + list(pieces) + list(state)
    stat = jax.ShapeDtypeStruct((1, width), jnp.float32)
    out_shape = [stat, stat, jax.ShapeDtypeStruct((head_size, width), jnp.float32)]
    scratch = [
        pltpu.VMEM((count, both_rows, head_size), jnp.bfloat16),
        pltpu.SMEM((count + 1,), jnp.int32),
    ]
    if theirs:
        scratch = [pltpu.VMEM(s.shape, s.dtype) for s in out_shape] + scratch
        out_shape = [jax.ShapeDtypeStruct((head_size + 16, width), jnp.bfloat16)]

    def body(*refs):
        attend_kernel(shifts, down, columns, len(state) > 0, theirs, heads, *refs)

    keys = count * both_rows // 2
    return pl.pallas_call(
        body,
        out_shape=out_shape,
        in_specs=[SM] + [VM] * (len(args) - 1),
        out_specs=[VM] * len(out_shape),
        scratch_shapes=scratch,
        compiler_params=PARAMS,
        cost_estimate=pl.CostEstimate(
            flops=4 * width * keys * head_size,
            bytes_accessed=4 * keys * head_size + 2 * width * head_size,
            transcendentals=width * keys,
        ),
    )(*args)


def combine_kernel(m_ref, l_ref, a_ref, p_ref, out_ref):
    depth = a_ref.shape[0]
    tail = p_ref[depth : depth + 16].astype(jnp.float32)
    level = tail[0:1] + tail[1:2] + tail[2:3]
    top = jnp.maximum(m_ref[...], level)
    here, there = jnp.exp2(m_ref[...] - top), jnp.exp2(level - top)
    whole = 1.0 / (l_ref[...] * here + there)
    mixed = a_ref[...] * (here * whole) + p_ref[:depth].astype(jnp.float32) * (there * whole)
    out_ref[...] = mixed.T.astype(jnp.bfloat16)


def combine(m, l, a, packet):
    return pl.pallas_call(
        combine_kernel,
        out_shape=jax.ShapeDtypeStruct(a.shape[::-1], jnp.bfloat16),
        in_specs=[VM] * 4,
        out_specs=VM,
        compiler_params=PARAMS,
    )(m, l, a, packet)


def local(queries, keys, values, span_order):
    rows, heads, head_size = queries.shape
    down, across = lax.axis_size("blk"), lax.axis_size("x")
    swap = [(0, 1), (1, 0)]
    own = queries.reshape(rows * heads, head_size)
    other = lax.ppermute(own, "core", swap)
    wide = (across, rows, head_size)
    k = jnp.broadcast_to(keys.reshape(1, rows, head_size), wide)
    v = jnp.broadcast_to(values.reshape(1, rows, head_size), wide)
    spread = jnp.concatenate([k, v], axis=1)
    row = lax.all_to_all(spread, "x", 0, 0, tiled=True)
    up = [(i, (i + 1) % down) for i in range(down)]
    back = [(i, (i - 1) % down) for i in range(down)]
    q = prepare(own, other)
    state = attend(span_order, q, [row], [0], (), heads, down)
    rising = falling = row
    for hop in range(1, down // 2):
        rising = lax.ppermute(rising, "blk", up)
        falling = lax.ppermute(falling, "blk", back)
        if hop <= 2:
            rising, state = lax.optimization_barrier((rising, state))
        state = attend(span_order, q, [rising, falling], [hop, down - hop], state, heads, down)
    farthest = lax.ppermute(rising, "blk", up)
    mine = q.shape[1] // 2
    half, other_half = (0, mine), (mine, 2 * mine)
    (packet,) = attend(
        span_order, q, [farthest], [down // 2], state, heads, down, other_half, True
    )
    packet, state = lax.optimization_barrier((packet, state))
    theirs = lax.ppermute(packet, "core", swap)
    m, l, a = attend(span_order, q, [farthest], [down // 2], state, heads, down, half)
    return combine(m, l, a, theirs).reshape(rows, heads, head_size)


def solution(mesh):
    blk, uly, tp = mesh.devices.shape
    fine = Mesh(mesh.devices.reshape(blk, uly // 2, 2, tp), ("blk", "x", "core", "tp"))
    spec = P(("blk", "x", "core"), "tp", None)
    return jax.shard_map(
        local, mesh=fine, in_specs=(spec, spec, spec, P()), out_specs=spec, check_vma=False
    )
```
